32 devices in a mesh: blk: 8 (over z, x), narrow: 4 (over y, core).
Axes of the slice: x: 2, y: 2, z: 4, core: 2. Of those that a mesh axis runs over, the one named last changes fastest.
Arguments:
- source: float32 [1024, 32, 128], P('blk', 'narrow'), may hold values from -6 to 6
- shift: float32 [1024, 32, 128], P('blk', 'narrow'), may hold values from 0.05 to 1
- start_field: float32 [1024, 32, 128], P('blk', 'narrow'), may hold values from -6 to 6
Outputs:
- field: float32 [1024, 32, 128], P('blk', 'narrow')
The draws below stay inside these ranges and needn't reach their ends.
All inputs are finite; a program needn't handle non-finite values.
Results may differ from the reference program's by a relative error of at most 0.0003.
Values sent between devices are 32-bit elements; how exact they have to be, the bound alone decides.
A program may use at most 64 MiB of HBM per device.

```python
import math
import jax
import jax.numpy as jnp
from jax import lax

CX = 128
CZ = 128
OV = 8
PASSES = 3
SWEEPS = 2
NX = 1024
NY = 32
N_BLK = 8


def shard_levels(own_key, shape, pieces, smallest, top_value):
    loudness = 1.0
    for position, shards_of in pieces:
        draws = jax.random.uniform(jax.random.fold_in(jax.random.fold_in(own_key, 6), position), (shards_of,), jnp.float32, smallest / len(pieces), top_value / len(pieces))
        loudness = loudness * jnp.repeat(jnp.exp(draws), shape[position] // shards_of).reshape((-1,) + (1,) * (len(shape) - 1 - position))
    return loudness


def bell_draw(key, extent, scale, limit, split=(), kind=jnp.bfloat16):
    array = jax.random.normal(key, extent, jnp.float32) * scale
    if len(split) > 0:
        array = shard_levels(key, extent, split, -0.22, 0.18) * array
    return jnp.clip(array, min=-limit, max=limit).astype(kind)


def setup_inputs(seed: int = 0) -> dict:
    keys = jax.random.split(jax.random.key(seed), 4)
    return {
        "source": bell_draw(keys[0], (NX, NY, CZ), 1.0, 6.0, ((0, 8), (1, 4)), jnp.float32),
        "shift": jnp.clip(jnp.exp(math.log(1.0) - 2.9957323 * jax.random.uniform(keys[1], (NX, NY, CZ), jnp.float32) ** shard_levels(keys[1], (NX, NY, CZ), ((0, 8), (1, 4)), -0.2, 0.2)), 0.05, 1.0),
        "start_field": bell_draw(keys[2], (NX, NY, CZ), 1.0, 6.0, ((0, 8), (1, 4)), jnp.float32),
    }


low_end = 0.05
high_end = 2.2
centre_weight = 1.0 + 1.0 / 7.0


def cheby_terms(passes):
    centre = (high_end + low_end) / 2.0
    half_width = (high_end - low_end) / 2.0
    sigma_value = centre / half_width
    ratio_now = 1.0 / sigma_value
    terms = []
    for repeat in range(passes):
        ratio_next = 1.0 / (2.0 * sigma_value - ratio_now)
        terms.append((ratio_next * ratio_now, 2.0 * ratio_next / half_width))
        ratio_now = ratio_next
    return centre, terms


def smooth(padded):
    along_x = 0.5 * (padded[:-2] + padded[2:]) + padded[1:-1]
    along_y = 0.5 * (along_x[:, :-2] + along_x[:, 2:]) + along_x[:, 1:-1]
    return 0.5 * (along_y[:, :, :-2] + along_y[:, :, 2:]) + along_y[:, :, 1:-1]


def operate(padded, shift):
    inner = padded[1:-1, 1:-1, 1:-1]
    return (centre_weight + shift) * inner - smooth(padded) / 7.0


def local_solve(residue, shift):
    centre, terms = cheby_terms(PASSES)
    direction = residue / centre
    update = direction
    for scale_old, scale_new in terms:
        image = operate(jnp.pad(direction, 1), shift)
        residue = residue - image
        direction = scale_old * direction + scale_new * residue
        update = update + direction
    return update


def global_apply(field, shift):
    wrapped = jnp.concatenate([field[-1:], field, field[:1]], axis=0)
    padded = jnp.pad(wrapped, ((0, 0), (1, 1), (1, 1)))
    return operate(padded, shift)


def wrap_margin(field):
    return jnp.concatenate([field[-OV:], field, field[:OV]], axis=0)


def spread(part, colour):
    empty = jnp.zeros_like(part)
    if colour == 0:
        paired = jnp.stack([part, empty], axis=1)
    else:
        paired = jnp.stack([empty, part], axis=1)
    return paired.reshape((N_BLK,) + part.shape[1:])


def reference(source, shift, start_field):
    field = start_field
    span = CX + 2 * OV
    half_count = N_BLK // 2
    shift_wrapped = wrap_margin(shift)
    for sweep in range(SWEEPS):
        for colour in range(2):
            residue = source - global_apply(field, shift)
            residue_wrapped = wrap_margin(residue)

            def solve_one(index):
                begin = ((2 * index + colour) * CX).astype(jnp.int32)
                piece = lax.dynamic_slice_in_dim(residue_wrapped, begin, span, 0)
                shift_piece = lax.dynamic_slice_in_dim(shift_wrapped, begin, span, 0)
                return local_solve(piece, shift_piece)

            updates = lax.map(solve_one, jnp.arange(half_count, dtype=jnp.int32))
            own_part = spread(updates[:, OV:OV + CX], colour)
            lower_part = spread(updates[:, :OV], colour)
            upper_part = spread(updates[:, OV + CX:], colour)
            correction = own_part.at[:, CX - OV:].add(jnp.roll(lower_part, -1, axis=0))
            correction = correction.at[:, :OV].add(jnp.roll(upper_part, 1, axis=0))
            field = field + correction.reshape(NX, NY, CZ)
    return field
```

```python
import jax
import jax.numpy as jnp
from jax import lax
from jax.experimental import pallas as pl
from jax.experimental.pallas import tpu as pltpu
from jax.sharding import PartitionSpec as P

OV = 8
PASSES = 3
SWEEPS = 2
HALO = PASSES + 1
UNROLL = 4
MESH = pl.DeviceIdType.MESH

low_end = 0.05
high_end = 2.2
centre_weight = 1.0 + 1.0 / 7.0

DIRECTIONS = [(0, 1), (0, -1), (1, 0), (-1, 0), (1, 1), (1, -1), (-1, 1), (-1, -1)]


def cheby_terms(passes):
    centre = (high_end + low_end) / 2.0
    half_width = (high_end - low_end) / 2.0
    sigma_value = centre / half_width
    ratio_now = 1.0 / sigma_value
    terms = []
    for repeat in range(passes):
        ratio_next = 1.0 / (2.0 * sigma_value - ratio_now)
        terms.append((ratio_next * ratio_now, 2.0 * ratio_next / half_width))
        ratio_now = ratio_next
    return centre, terms


def kernel(
    source, shift, start, out,
    F, S, C, R0, R1, R2, D1, D2, X, Y,
    own_sem, out_sem, init_send, init_recv, x_send, x_recv, f_send, f_recv,
    y_send, y_recv, last_send, last_recv,
):
    n, ny, nz = source.shape
    blocks, bands = lax.axis_size("blk"), lax.axis_size("narrow")
    b, w = lax.axis_index("blk"), lax.axis_index("narrow")
    base = OV + 1
    edge = 2 * OV + 1
    has_low, has_high = w > 0, w < bands - 1
    inv_c = 1.0 / cheby_terms(PASSES)[0]
    terms = cheby_terms(PASSES)[1]

    def device(dx, dy):
        return (lax.rem(b + dx + blocks, blocks), w + dy)

    def when_to(dy, act):
        if dy == 0:
            act()
        else:
            pl.when(has_high if dy > 0 else has_low)(act)

    def when_from(dy, act):
        when_to(-dy, act)

    zero_rows = jnp.zeros((2 * HALO + ny, nz), jnp.float32)

    def clear(refs, first, last):
        def body(i, carry):
            for ref in refs:
                ref[i] = zero_rows
            return carry
        lax.fori_loop(first, last, body, 0)

    clear((R0, D1, D2), 0, n + 2 * base)

    @pl.when(jnp.logical_or(w == 0, w == bands - 1))
    def _():
        clear((F, S, C), 0, n + 2 * base)

        def body_x(i, carry):
            for k in range(X.shape[0]):
                X[k, i] = zero_rows
            return carry

        lax.fori_loop(0, edge, body_x, 0)

        def body_y(i, carry):
            for k in range(Y.shape[0]):
                Y[k, i] = jnp.zeros((2 * HALO, nz), jnp.float32)
            return carry
        lax.fori_loop(0, Y.shape[1], body_y, 0)

    own = [
        pltpu.make_async_copy(
            array, buf.at[pl.ds(base, n), pl.ds(HALO, ny)], own_sem.at[k])
        for k, (array, buf) in enumerate(((start, F), (source, S), (shift, C)))
    ]
    for copy in own:
        copy.start()

    barrier = pltpu.get_barrier_semaphore()
    for dx, dy in DIRECTIONS:
        def greet(dx=dx, dy=dy):
            pl.semaphore_signal(barrier, inc=1, device_id=device(dx, dy), device_id_type=MESH)
        when_to(dy, greet)
    pl.semaphore_wait(barrier, 2 + 3 * jnp.where(has_low, 1, 0) + 3 * jnp.where(has_high, 1, 0))

    def rows_of(dy, depth):
        if dy == 0:
            return pl.ds(0, ny), pl.ds(HALO, ny)
        if dy > 0:
            return pl.ds(ny - depth, depth), pl.ds(HALO - depth, depth)
        return pl.ds(0, depth), pl.ds(HALO + ny, depth)

    def layers_of(dx, width):
        if dx == 0:
            return pl.ds(0, n), pl.ds(base, n)
        if dx > 0:
            return pl.ds(n - width, width), pl.ds(base - width, width)
        return pl.ds(0, width), pl.ds(base + n, width)

    def initial(array_index, k):
        dx, dy = DIRECTIONS[k]
        array, buf = ((start, F), (source, S), (shift, C))[array_index]
        wide, deep = (OV + 1, HALO) if array_index == 0 else (OV, HALO - 1)
        from_rows, to_rows = rows_of(dy, deep)
        from_layers, to_layers = layers_of(dx, wide)
        return pltpu.make_async_remote_copy(
            src_ref=array.at[from_layers, from_rows],
            dst_ref=buf.at[to_layers, to_rows],
            send_sem=init_send.at[array_index, k],
            recv_sem=init_recv.at[array_index, k],
            device_id=device(dx, dy), device_id_type=MESH)

    even = lax.rem(b, 2) == 0
    odd = lax.rem(b, 2) == 1

    def all_initial(dirs, field_margin, start_it, send_wait=False):
        for array_index in range(3):
            for k in dirs:
                dx, dy = DIRECTIONS[k]
                if array_index == 0 and dx != 0 and not field_margin:
                    continue
                copy = initial(array_index, k)
                if start_it:
                    when_to(dy, copy.start)
                elif send_wait:
                    when_to(dy, copy.wait_send)
                else:
                    when_from(dy, copy.wait_recv)

    side_dirs, cross_dirs = (0, 1), (2, 3, 4, 5, 6, 7)

    lane = lax.broadcasted_iota(jnp.int32, (8, nz), 1)
    first_lane, last_lane = lane == 0, lane == nz - 1
    row = lax.broadcasted_iota(jnp.int32, (8, nz), 0)

    def weight(top):
        place = w * ny - HALO + top + row
        inside = jnp.logical_and(place >= 0, place < bands * ny)
        return jnp.where(inside, jnp.float32(1.0 / 56.0), jnp.float32(0.0))

    def filter_rows(ref, x, top):
        mid = ref[x, pl.ds(top, 8)]
        return (ref[x, pl.ds(top - 1, 8)] + ref[x, pl.ds(top + 1, 8)]) + (mid + mid)

    def stencil(ref, first, last, tops, emit):
        carry = []
        for top in tops:
            below, here = filter_rows(ref, first - 1, top), filter_rows(ref, first, top)
            carry += [below + here, here]

        def layer(x, carry):
            carry = list(carry)
            for t, top in enumerate(tops):
                pair, here = carry[2 * t], carry[2 * t + 1]
                above = filter_rows(ref, x + 1, top)
                next_pair = here + above
                both = pair + next_pair
                left = jnp.where(first_lane, 0.0, pltpu.roll(both, 1, 1))
                right = jnp.where(last_lane, 0.0, pltpu.roll(both, nz - 1, 1))
                emit(x, top, t, (both + both) + (left + right))
                carry[2 * t], carry[2 * t + 1] = next_pair, above
            return tuple(carry)

        whole = (last - first) // UNROLL

        def body(i, carry):
            for u in range(UNROLL):
                carry = layer(first + i * UNROLL + u, carry)
            return carry

        carry = lax.fori_loop(0, whole, body, tuple(carry))
        for x in range(first + whole * UNROLL, last):
            carry = layer(x, carry)

    wide_tops, own_tops = (1, 2 * HALO + ny - 9), (HALO,)
    wide_weights, own_weights = [weight(t) for t in wide_tops], [weight(t) for t in own_tops]

    def residual(first, last):
        def emit(x, top, t, filtered):
            here = pl.ds(top, 8)
            R0[x, here] = (S[x, here] - (centre_weight + C[x, here]) * F[x, here]) + wide_weights[t] * filtered
        stencil(F, first, last, wide_tops, emit)

    def pass_one(first, last):
        p, q = terms[0]
        def emit(x, top, t, filtered):
            here = pl.ds(top, 8)
            r = R0[x, here]
            image = (centre_weight + C[x, here]) * r - wide_weights[t] * filtered
            r1 = r - inv_c * image
            R1[x, here] = r1
            D1[x, here] = (p * inv_c) * r + q * r1
        stencil(R0, first, last, wide_tops, emit)

    def pass_two(first, last):
        p, q = terms[1]
        def emit(x, top, t, filtered):
            here = pl.ds(top, 8)
            d = D1[x, here]
            r2 = R1[x, here] - ((centre_weight + C[x, here]) * d - wide_weights[t] * filtered)
            R2[x, here] = r2
            D2[x, here] = p * d + q * r2
        stencil(D1, first, last, wide_tops, emit)

    def pass_three(first, last):
        p, q = terms[2]
        def emit(x, top, t, filtered):
            here = pl.ds(top, 8)
            d = D2[x, here]
            r3 = R2[x, here] - ((centre_weight + C[x, here]) * d - own_weights[t] * filtered)
            update = (inv_c * R0[x, here] + D1[x, here]) + (d + (p * d + q * r3))
            F[x, here] = F[x, here] + update
        stencil(D2, first, last, own_tops, emit)

    end = n + 2 * base - 1
    inner = 2 * OV + 2
    outer = end + 1 - inner

    def solve_inside():
        residual(inner, outer)
        pass_one(inner + 1, outer - 1)
        pass_two(inner + 2, outer - 2)
        pass_three(inner + 3, outer - 3)

    def solve_edges():
        for k, run in enumerate((residual, pass_one, pass_two, pass_three)):
            run(1, inner + k)
            run(outer - k, end)

    def across(e, side):
        dx = 1 if side == 0 else -1
        begin = base + n - OV - 1 if dx > 0 else 1
        return pltpu.make_async_remote_copy(
            src_ref=F.at[pl.ds(begin, edge), pl.ds(HALO, ny)],
            dst_ref=X.at[2 * e + side, :, pl.ds(HALO, ny)],
            send_sem=x_send.at[e, side], recv_sem=x_recv.at[e, side],
            device_id=device(dx, 0), device_id_type=MESH)

    def forward(e, side, dy):
        from_row = HALO + ny - HALO if dy > 0 else HALO
        to_row = 0 if dy > 0 else HALO + ny
        k = 2 * side + (0 if dy > 0 else 1)
        return pltpu.make_async_remote_copy(
            src_ref=X.at[2 * e + side, :, pl.ds(from_row, HALO)],
            dst_ref=X.at[2 * e + side, :, pl.ds(to_row, HALO)],
            send_sem=f_send.at[e, k], recv_sem=f_recv.at[e, k],
            device_id=device(0, dy), device_id_type=MESH)

    keep = n - 2 * OV

    def along(e, dy):
        from_row = HALO + ny - HALO if dy > 0 else HALO
        to_row = 0 if dy > 0 else HALO
        k = 0 if dy > 0 else 1
        return pltpu.make_async_remote_copy(
            src_ref=F.at[pl.ds(base + OV, keep), pl.ds(from_row, HALO)],
            dst_ref=Y.at[e, :, pl.ds(to_row, HALO)],
            send_sem=y_send.at[e, k], recv_sem=y_recv.at[e, k],
            device_id=device(0, dy), device_id_type=MESH)

    def last_copy(side):
        dx = 1 if side == 0 else -1
        begin = base + n if dx > 0 else base - OV
        return pltpu.make_async_remote_copy(
            src_ref=F.at[pl.ds(begin, OV), pl.ds(HALO, ny)],
            dst_ref=X.at[side + 2 * (2 * SWEEPS - 1), pl.ds(0, OV), pl.ds(HALO, ny)],
            send_sem=last_send.at[side], recv_sem=last_recv.at[side],
            device_id=device(dx, 0), device_id_type=MESH)

    def send_after(e):
        for side in (0, 1):
            across(e, side).start()
        if e < 2 * SWEEPS - 2:
            for dy in (1, -1):
                when_to(dy, along(e, dy).start)

    def finish_sends(e):
        for side in (0, 1):
            across(e, side).wait_send()
        if e < 2 * SWEEPS - 2:
            for dy in (1, -1):
                when_to(dy, along(e, dy).wait_send)

    def take_halo(e):
        for dy in (1, -1):
            when_from(dy, along(e, dy).wait_recv)

        def body(i, carry):
            F[base + OV + i, pl.ds(0, HALO)] = Y[e, i, pl.ds(0, HALO)]
            F[base + OV + i, pl.ds(HALO + ny, HALO)] = Y[e, i, pl.ds(HALO, HALO)]
            return carry
        lax.fori_loop(0, keep, body, 0)

    def take_margins(e):
        for side in (0, 1):
            across(e, side).wait_recv()
            for dy in (1, -1):
                when_to(dy, forward(e, side, dy).start)
        for side in (0, 1):
            for dy in (1, -1):
                when_from(dy, forward(e, side, dy).wait_recv)

        def body(i, carry):
            F[i] = X[2 * e, i]
            F[base + n - OV + i] = X[2 * e + 1, i]
            return carry
        lax.fori_loop(0, edge, body, 0)
        for side in (0, 1):
            for dy in (1, -1):
                when_to(dy, forward(e, side, dy).wait_send)

    def write_out(first, count, k):
        return pltpu.make_async_copy(
            F.at[pl.ds(base + first, count), pl.ds(HALO, ny)],
            out.at[pl.ds(first, count)], out_sem.at[k])

    all_initial(side_dirs, True, True)

    @pl.when(even)
    def _():
        all_initial(cross_dirs, False, True)
        for copy in own:
            copy.wait()
        all_initial(side_dirs, True, False)
        solve_inside()
        all_initial(cross_dirs, True, False)
        solve_edges()
        send_after(0)
        all_initial(side_dirs, True, False, True)
        all_initial(cross_dirs, False, False, True)
        for sweep in range(1, SWEEPS):
            e = 2 * sweep
            finish_sends(e - 2)
            take_halo(e - 2)
            solve_inside()
            take_margins(e - 1)
            solve_edges()
            send_after(e)
        finish_sends(2 * SWEEPS - 2)
        middle = write_out(OV, n - 2 * OV, 0)
        middle.start()
        for side in (0, 1):
            last_copy(side).wait_recv()

        def body(i, carry):
            here = pl.ds(HALO, ny)
            F[base + i, here] = X[2 * (2 * SWEEPS - 1), i, here]
            F[base + n - OV + i, here] = X[2 * (2 * SWEEPS - 1) + 1, i, here]
            return carry
        lax.fori_loop(0, OV, body, 0)
        low, high = write_out(0, OV, 1), write_out(n - OV, OV, 2)
        low.start()
        high.start()
        middle.wait()
        low.wait()
        high.wait()

    @pl.when(odd)
    def _():
        all_initial(cross_dirs, True, True)
        for copy in own:
            copy.wait()
        all_initial(side_dirs, True, False)
        solve_inside()
        all_initial(cross_dirs, False, False)
        all_initial(side_dirs, True, False, True)
        all_initial(cross_dirs, True, False, True)
        for sweep in range(SWEEPS):
            e = 2 * sweep + 1
            if sweep > 0:
                finish_sends(e - 2)
                take_halo(e - 2)
                solve_inside()
            take_margins(e - 1)
            solve_edges()
            if sweep < SWEEPS - 1:
                send_after(e)
        for side in (0, 1):
            last_copy(side).start()
        whole = write_out(0, n, 0)
        whole.start()
        for side in (0, 1):
            last_copy(side).wait_send()
        whole.wait()


def per_device(source, shift, start_field):
    n, ny, nz = source.shape
    layers, rows = n + 2 * OV + 2, ny + 2 * HALO
    work = pltpu.VMEM((layers, rows, nz), jnp.float32)
    dma = pltpu.SemaphoreType.DMA
    phases = 2 * SWEEPS
    return pl.pallas_call(
        kernel,
        out_shape=jax.ShapeDtypeStruct(source.shape, source.dtype),
        in_specs=[pl.BlockSpec(memory_space=pl.ANY)] * 3,
        out_specs=pl.BlockSpec(memory_space=pl.ANY),
        scratch_shapes=[work] * 8 + [
            pltpu.VMEM((2 * phases, 2 * OV + 1, rows, nz), jnp.float32),
            pltpu.VMEM((phases - 2, n - 2 * OV, 2 * HALO, nz), jnp.float32),
            dma((3,)), dma((3,)),
            dma((3, 8)), dma((3, 8)),
            dma((phases - 1, 2)), dma((phases - 1, 2)),
            dma((phases - 1, 4)), dma((phases - 1, 4)),
            dma((phases - 2, 2)), dma((phases - 2, 2)),
            dma((2,)), dma((2,)),
        ],
        compiler_params=pltpu.CompilerParams(
            collective_id=0, has_side_effects=True, vmem_limit_bytes=32 * 2**20),
    )(source, shift, start_field)


def solution(mesh):
    placed = P("blk", "narrow", None)
    return jax.shard_map(
        per_device, mesh=mesh, in_specs=(placed,) * 3, out_specs=placed, check_vma=False
    )
```

```python
import jax
import jax.numpy as jnp
from jax import lax
from jax.experimental import pallas as pl
from jax.experimental.pallas import tpu as pltpu
from jax.sharding import PartitionSpec as P

OV = 8
PASSES = 3
SWEEPS = 2
HALO = PASSES + 1
UNROLL = 20
MESH = pl.DeviceIdType.MESH

low_end = 0.05
high_end = 2.2
centre_weight = 1.0 + 1.0 / 7.0

DIRECTIONS = [(0, 1), (0, -1), (1, 0), (-1, 0), (1, 1), (1, -1), (-1, 1), (-1, -1)]


def cheby_terms(passes):
    centre = (high_end + low_end) / 2.0
    half_width = (high_end - low_end) / 2.0
    sigma_value = centre / half_width
    ratio_now = 1.0 / sigma_value
    terms = []
    for repeat in range(passes):
        ratio_next = 1.0 / (2.0 * sigma_value - ratio_now)
        terms.append((ratio_next * ratio_now, 2.0 * ratio_next / half_width))
        ratio_now = ratio_next
    return centre, terms


def kernel(
    source, shift, start, out,
    F, S, C, R0, R1, R2, D1, D2, X, Y,
    own_sem, out_sem, init_send, init_recv, x_send, x_recv, f_send, f_recv,
    y_send, y_recv, last_send, last_recv,
):
    n, ny, nz = source.shape
    blocks, bands = lax.axis_size("blk"), lax.axis_size("narrow")
    b, w = lax.axis_index("blk"), lax.axis_index("narrow")
    base = OV + 1
    edge = 2 * OV + 1
    has_low, has_high = w > 0, w < bands - 1
    inv_c = 1.0 / cheby_terms(PASSES)[0]
    terms = cheby_terms(PASSES)[1]

    def device(dx, dy):
        return (lax.rem(b + dx + blocks, blocks), w + dy)

    def when_to(dy, act):
        if dy == 0:
            act()
        else:
            pl.when(has_high if dy > 0 else has_low)(act)

    def when_from(dy, act):
        when_to(-dy, act)

    zero_rows = jnp.zeros((2 * HALO + ny, nz), jnp.float32)

    def clear(refs, first, last):
        def body(i, carry):
            for ref in refs:
                ref[i] = zero_rows
            return carry
        lax.fori_loop(first, last, body, 0)

    clear((R0, D1, D2), 0, n + 2 * base)

    @pl.when(jnp.logical_or(w == 0, w == bands - 1))
    def _():
        clear((F, S, C), 0, n + 2 * base)

        def body_x(i, carry):
            for k in range(X.shape[0]):
                X[k, i] = zero_rows
            return carry

        lax.fori_loop(0, edge, body_x, 0)

        def body_y(i, carry):
            for k in range(Y.shape[0]):
                Y[k, i] = jnp.zeros((2 * HALO, nz), jnp.float32)
            return carry
        lax.fori_loop(0, Y.shape[1], body_y, 0)

    own = [
        pltpu.make_async_copy(
            array, buf.at[pl.ds(base, n), pl.ds(HALO, ny)], own_sem.at[k])
        for k, (array, buf) in enumerate(((start, F), (source, S), (shift, C)))
    ]
    for copy in own:
        copy.start()

    barrier = pltpu.get_barrier_semaphore()
    for dx, dy in DIRECTIONS:
        def greet(dx=dx, dy=dy):
            pl.semaphore_signal(barrier, inc=1, device_id=device(dx, dy), device_id_type=MESH)
        when_to(dy, greet)
    pl.semaphore_wait(barrier, 2 + 3 * jnp.where(has_low, 1, 0) + 3 * jnp.where(has_high, 1, 0))

    def rows_of(dy, depth):
        if dy == 0:
            return pl.ds(0, ny), pl.ds(HALO, ny)
        if dy > 0:
            return pl.ds(ny - depth, depth), pl.ds(HALO - depth, depth)
        return pl.ds(0, depth), pl.ds(HALO + ny, depth)

    def layers_of(dx, width):
        if dx == 0:
            return pl.ds(0, n), pl.ds(base, n)
        if dx > 0:
            return pl.ds(n - width, width), pl.ds(base - width, width)
        return pl.ds(0, width), pl.ds(base + n, width)

    def initial(array_index, k):
        dx, dy = DIRECTIONS[k]
        array, buf = ((start, F), (source, S), (shift, C))[array_index]
        wide, deep = (OV + 1, HALO) if array_index == 0 else (OV, HALO - 1)
        from_rows, to_rows = rows_of(dy, deep)
        from_layers, to_layers = layers_of(dx, wide)
        return pltpu.make_async_remote_copy(
            src_ref=array.at[from_layers, from_rows],
            dst_ref=buf.at[to_layers, to_rows],
            send_sem=init_send.at[array_index, k],
            recv_sem=init_recv.at[array_index, k],
            device_id=device(dx, dy), device_id_type=MESH)

    even = lax.rem(b, 2) == 0
    odd = lax.rem(b, 2) == 1

    def all_initial(dirs, field_margin, start_it, send_wait=False):
        for array_index in range(3):
            for k in dirs:
                dx, dy = DIRECTIONS[k]
                if array_index == 0 and dx != 0 and not field_margin:
                    continue
                copy = initial(array_index, k)
                if start_it:
                    when_to(dy, copy.start)
                elif send_wait:
                    when_to(dy, copy.wait_send)
                else:
                    when_from(dy, copy.wait_recv)

    side_dirs, cross_dirs = (0, 1), (2, 3, 4, 5, 6, 7)

    lane = lax.broadcasted_iota(jnp.int32, (8, nz), 1)
    first_lane, last_lane = lane == 0, lane == nz - 1
    row = lax.broadcasted_iota(jnp.int32, (8, nz), 0)

    def weight(top):
        place = w * ny - HALO + top + row
        inside = jnp.logical_and(place >= 0, place < bands * ny)
        return jnp.where(inside, jnp.float32(1.0 / 56.0), jnp.float32(0.0))

    def filter_rows(ref, x, top):
        mid = ref[x, pl.ds(top, 8)]
        return (ref[x, pl.ds(top - 1, 8)] + ref[x, pl.ds(top + 1, 8)]) + (mid + mid)

    def stencil(ref, first, last, tops, emit):
        carry = []
        for top in tops:
            below, here = filter_rows(ref, first - 1, top), filter_rows(ref, first, top)
            carry += [below + here, here]

        def layer(x, carry):
            carry = list(carry)
            for t, top in enumerate(tops):
                pair, here = carry[2 * t], carry[2 * t + 1]
                above = filter_rows(ref, x + 1, top)
                next_pair = here + above
                both = pair + next_pair
                left = jnp.where(first_lane, 0.0, pltpu.roll(both, 1, 1))
                right = jnp.where(last_lane, 0.0, pltpu.roll(both, nz - 1, 1))
                emit(x, top, t, (both + both) + (left + right))
                carry[2 * t], carry[2 * t + 1] = next_pair, above
            return tuple(carry)

        whole = (last - first) // UNROLL

        def body(i, carry):
            for u in range(UNROLL):
                carry = layer(first + i * UNROLL + u, carry)
            return carry

        carry = lax.fori_loop(0, whole, body, tuple(carry))
        for x in range(first + whole * UNROLL, last):
            carry = layer(x, carry)

    wide_tops, own_tops = (1, 2 * HALO + ny - 9), (HALO,)
    wide_weights, own_weights = [weight(t) for t in wide_tops], [weight(t) for t in own_tops]

    def residual(first, last):
        def emit(x, top, t, filtered):
            here = pl.ds(top, 8)
            R0[x, here] = (S[x, here] - (centre_weight + C[x, here]) * F[x, here]) + wide_weights[t] * filtered
        stencil(F, first, last, wide_tops, emit)

    def pass_one(first, last):
        p, q = terms[0]
        def emit(x, top, t, filtered):
            here = pl.ds(top, 8)
            r = R0[x, here]
            image = (centre_weight + C[x, here]) * r - wide_weights[t] * filtered
            r1 = r - inv_c * image
            R1[x, here] = r1
            D1[x, here] = (p * inv_c) * r + q * r1
        stencil(R0, first, last, wide_tops, emit)

    def pass_two(first, last):
        p, q = terms[1]
        def emit(x, top, t, filtered):
            here = pl.ds(top, 8)
            d = D1[x, here]
            r2 = R1[x, here] - ((centre_weight + C[x, here]) * d - wide_weights[t] * filtered)
            R2[x, here] = r2
            D2[x, here] = p * d + q * r2
        stencil(D1, first, last, wide_tops, emit)

    def pass_three(first, last):
        p, q = terms[2]
        def emit(x, top, t, filtered):
            here = pl.ds(top, 8)
            d = D2[x, here]
            r3 = R2[x, here] - ((centre_weight + C[x, here]) * d - own_weights[t] * filtered)
            update = (inv_c * R0[x, here] + D1[x, here]) + (d + (p * d + q * r3))
            F[x, here] = F[x, here] + update
        stencil(D2, first, last, own_tops, emit)

    end = n + 2 * base - 1
    inner = 2 * OV + 2
    outer = end + 1 - inner

    def solve_inside():
        residual(inner, outer)
        pass_one(inner + 1, outer - 1)
        pass_two(inner + 2, outer - 2)
        pass_three(inner + 3, outer - 3)

    def solve_edge(side):
        for k, run in enumerate((residual, pass_one, pass_two, pass_three)):
            if side == 0:
                run(1, inner + k)
            else:
                run(outer - k, end)

    def across(e, side):
        dx = 1 if side == 0 else -1
        begin = base + n - OV - 1 if dx > 0 else 1
        return pltpu.make_async_remote_copy(
            src_ref=F.at[pl.ds(begin, edge), pl.ds(HALO, ny)],
            dst_ref=X.at[2 * e + side, :, pl.ds(HALO, ny)],
            send_sem=x_send.at[e, side], recv_sem=x_recv.at[e, side],
            device_id=device(dx, 0), device_id_type=MESH)

    def forward(e, side, dy):
        from_row = HALO + ny - HALO if dy > 0 else HALO
        to_row = 0 if dy > 0 else HALO + ny
        k = 2 * side + (0 if dy > 0 else 1)
        return pltpu.make_async_remote_copy(
            src_ref=X.at[2 * e + side, :, pl.ds(from_row, HALO)],
            dst_ref=X.at[2 * e + side, :, pl.ds(to_row, HALO)],
            send_sem=f_send.at[e, k], recv_sem=f_recv.at[e, k],
            device_id=device(0, dy), device_id_type=MESH)

    keep = n - 2 * OV

    def along(e, dy):
        from_row = HALO + ny - HALO if dy > 0 else HALO
        to_row = 0 if dy > 0 else HALO
        k = 0 if dy > 0 else 1
        return pltpu.make_async_remote_copy(
            src_ref=F.at[pl.ds(base + OV, keep), pl.ds(from_row, HALO)],
            dst_ref=Y.at[e, :, pl.ds(to_row, HALO)],
            send_sem=y_send.at[e, k], recv_sem=y_recv.at[e, k],
            device_id=device(0, dy), device_id_type=MESH)

    def last_copy(side):
        dx = 1 if side == 0 else -1
        begin = base + n if dx > 0 else base - OV
        return pltpu.make_async_remote_copy(
            src_ref=F.at[pl.ds(begin, OV), pl.ds(HALO, ny)],
            dst_ref=X.at[side + 2 * (2 * SWEEPS - 1), pl.ds(0, OV), pl.ds(HALO, ny)],
            send_sem=last_send.at[side], recv_sem=last_recv.at[side],
            device_id=device(dx, 0), device_id_type=MESH)

    def send_halo(e):
        if e < 2 * SWEEPS - 2:
            for dy in (1, -1):
                when_to(dy, along(e, dy).start)

    def finish_sends(e):
        for side in (0, 1):
            across(e, side).wait_send()
        if e < 2 * SWEEPS - 2:
            for dy in (1, -1):
                when_to(dy, along(e, dy).wait_send)

    def take_halo(e):
        for dy in (1, -1):
            when_from(dy, along(e, dy).wait_recv)

        def body(i, carry):
            F[base + OV + i, pl.ds(0, HALO)] = Y[e, i, pl.ds(0, HALO)]
            F[base + OV + i, pl.ds(HALO + ny, HALO)] = Y[e, i, pl.ds(HALO, HALO)]
            return carry
        lax.fori_loop(0, keep, body, 0)

    def send_side(e, side):
        across(e, 1 - side).start()

    def pass_margin_on(e, side):
        across(e, side).wait_recv()
        for dy in (1, -1):
            when_to(dy, forward(e, side, dy).start)

    def take_margin(e, side):
        for dy in (1, -1):
            when_from(dy, forward(e, side, dy).wait_recv)
        begin = 0 if side == 0 else base + n - OV
        for i in range(edge):
            F[begin + i] = X[2 * e + side, i]

    def margins_done(e):
        for side in (0, 1):
            for dy in (1, -1):
                when_to(dy, forward(e, side, dy).wait_send)

    def step(e, order, send):
        for side in order:
            pass_margin_on(e - 1, side)
        for side in order:
            take_margin(e - 1, side)
            solve_edge(side)
            send(side)

    def write_out(first, count, k):
        return pltpu.make_async_copy(
            F.at[pl.ds(base + first, count), pl.ds(HALO, ny)],
            out.at[pl.ds(first, count)], out_sem.at[k])

    all_initial(side_dirs, True, True)

    @pl.when(even)
    def _():
        all_initial(cross_dirs, False, True)
        for copy in own:
            copy.wait()
        all_initial(side_dirs, True, False)
        solve_inside()
        all_initial(cross_dirs, True, False)
        for side in (0, 1):
            solve_edge(side)
            send_side(0, side)
        send_halo(0)
        all_initial(side_dirs, True, False, True)
        all_initial(cross_dirs, False, False, True)
        for sweep in range(1, SWEEPS):
            e = 2 * sweep
            finish_sends(e - 2)
            take_halo(e - 2)
            solve_inside()
            step(e, (0, 1), lambda side: send_side(e, side))
            send_halo(e)
            margins_done(e - 1)
        finish_sends(2 * SWEEPS - 2)
        middle = write_out(OV, n - 2 * OV, 0)
        middle.start()
        for side in (0, 1):
            last_copy(side).wait_recv()

        def body(i, carry):
            here = pl.ds(HALO, ny)
            F[base + i, here] = X[2 * (2 * SWEEPS - 1), i, here]
            F[base + n - OV + i, here] = X[2 * (2 * SWEEPS - 1) + 1, i, here]
            return carry
        lax.fori_loop(0, OV, body, 0)
        low, high = write_out(0, OV, 1), write_out(n - OV, OV, 2)
        low.start()
        high.start()
        middle.wait()
        low.wait()
        high.wait()

    @pl.when(odd)
    def _():
        all_initial(cross_dirs, True, True)
        for copy in own:
            copy.wait()
        all_initial(side_dirs, True, False)
        solve_inside()
        all_initial(cross_dirs, False, False)
        all_initial(side_dirs, True, False, True)
        all_initial(cross_dirs, True, False, True)
        for sweep in range(SWEEPS):
            e = 2 * sweep + 1
            if sweep > 0:
                finish_sends(e - 2)
                take_halo(e - 2)
                solve_inside()
            if sweep < SWEEPS - 1:
                step(e, (1, 0), lambda side: send_side(e, side))
                send_halo(e)
            else:
                step(e, (1, 0), lambda side: last_copy(1 - side).start())
            margins_done(e - 1)
        whole = write_out(0, n, 0)
        whole.start()
        for side in (0, 1):
            last_copy(side).wait_send()
        whole.wait()


def per_device(source, shift, start_field):
    n, ny, nz = source.shape
    layers, rows = n + 2 * OV + 2, ny + 2 * HALO
    work = pltpu.VMEM((layers, rows, nz), jnp.float32)
    dma = pltpu.SemaphoreType.DMA
    phases = 2 * SWEEPS
    return pl.pallas_call(
        kernel,
        out_shape=jax.ShapeDtypeStruct(source.shape, source.dtype),
        in_specs=[pl.BlockSpec(memory_space=pl.ANY)] * 3,
        out_specs=pl.BlockSpec(memory_space=pl.ANY),
        scratch_shapes=[work] * 8 + [
            pltpu.VMEM((2 * phases, 2 * OV + 1, rows, nz), jnp.float32),
            pltpu.VMEM((phases - 2, n - 2 * OV, 2 * HALO, nz), jnp.float32),
            dma((3,)), dma((3,)),
            dma((3, 8)), dma((3, 8)),
            dma((phases - 1, 2)), dma((phases - 1, 2)),
            dma((phases - 1, 4)), dma((phases - 1, 4)),
            dma((phases - 2, 2)), dma((phases - 2, 2)),
            dma((2,)), dma((2,)),
        ],
        compiler_params=pltpu.CompilerParams(
            collective_id=0, has_side_effects=True, vmem_limit_bytes=58 * 2**20),
    )(source, shift, start_field)


def solution(mesh):
    placed = P("blk", "narrow", None)
    return jax.shard_map(
        per_device, mesh=mesh, in_specs=(placed,) * 3, out_specs=placed, check_vma=False
    )
```

```python
import jax
import jax.numpy as jnp
from jax import lax
from jax.experimental import pallas as pl
from jax.experimental.pallas import tpu as pltpu
from jax.sharding import PartitionSpec as P

OV = 8
PASSES = 3
SWEEPS = 2
HALO = PASSES + 1
UNROLL = 20
MESH = pl.DeviceIdType.MESH

low_end = 0.05
high_end = 2.2
centre_weight = 1.0 + 1.0 / 7.0

DIRECTIONS = [(0, 1), (0, -1), (1, 0), (-1, 0), (1, 1), (1, -1), (-1, 1), (-1, -1)]


def cheby_terms(passes):
    centre = (high_end + low_end) / 2.0
    half_width = (high_end - low_end) / 2.0
    sigma_value = centre / half_width
    ratio_now = 1.0 / sigma_value
    terms = []
    for repeat in range(passes):
        ratio_next = 1.0 / (2.0 * sigma_value - ratio_now)
        terms.append((ratio_next * ratio_now, 2.0 * ratio_next / half_width))
        ratio_now = ratio_next
    return centre, terms


def kernel(
    source, shift, start, out,
    F, S, C, R0, R1, R2, D1, D2, X, Y,
    own_sem, out_sem, init_send, init_recv, x_send, x_recv, f_send, f_recv,
    y_send, y_recv, last_send, last_recv,
):
    n, ny, nz = source.shape
    blocks, bands = lax.axis_size("blk"), lax.axis_size("narrow")
    b, w = lax.axis_index("blk"), lax.axis_index("narrow")
    base = OV + 1
    edge = 2 * OV + 1
    has_low, has_high = w > 0, w < bands - 1
    inv_c = 1.0 / cheby_terms(PASSES)[0]
    terms = cheby_terms(PASSES)[1]

    def device(dx, dy):
        return (lax.rem(b + dx + blocks, blocks), w + dy)

    def when_to(dy, act):
        if dy == 0:
            act()
        else:
            pl.when(has_high if dy > 0 else has_low)(act)

    def when_from(dy, act):
        when_to(-dy, act)

    zero_rows = jnp.zeros((2 * HALO + ny, nz), jnp.float32)

    def clear(refs, first, last):
        def body(i, carry):
            for ref in refs:
                ref[i] = zero_rows
            return carry
        lax.fori_loop(first, last, body, 0)

    clear((R0, D1, D2), 0, n + 2 * base)

    @pl.when(jnp.logical_or(w == 0, w == bands - 1))
    def _():
        clear((F, S, C), 0, n + 2 * base)

        def body_x(i, carry):
            for k in range(X.shape[0]):
                X[k, i] = zero_rows
            return carry

        lax.fori_loop(0, edge, body_x, 0)

        def body_y(i, carry):
            for k in range(Y.shape[0]):
                Y[k, i] = jnp.zeros((2 * HALO, nz), jnp.float32)
            return carry
        lax.fori_loop(0, Y.shape[1], body_y, 0)

    own = [
        pltpu.make_async_copy(
            array, buf.at[pl.ds(base, n), pl.ds(HALO, ny)], own_sem.at[k])
        for k, (array, buf) in enumerate(((start, F), (source, S), (shift, C)))
    ]
    for copy in own:
        copy.start()

    barrier = pltpu.get_barrier_semaphore()
    for dx, dy in DIRECTIONS:
        def greet(dx=dx, dy=dy):
            pl.semaphore_signal(barrier, inc=1, device_id=device(dx, dy), device_id_type=MESH)
        when_to(dy, greet)
    pl.semaphore_wait(barrier, 2 + 3 * jnp.where(has_low, 1, 0) + 3 * jnp.where(has_high, 1, 0))

    def rows_of(dy, depth):
        if dy == 0:
            return pl.ds(0, ny), pl.ds(HALO, ny)
        if dy > 0:
            return pl.ds(ny - depth, depth), pl.ds(HALO - depth, depth)
        return pl.ds(0, depth), pl.ds(HALO + ny, depth)

    def layers_of(dx, width):
        if dx == 0:
            return pl.ds(0, n), pl.ds(base, n)
        if dx > 0:
            return pl.ds(n - width, width), pl.ds(base - width, width)
        return pl.ds(0, width), pl.ds(base + n, width)

    def initial(array_index, k):
        dx, dy = DIRECTIONS[k]
        array, buf = ((start, F), (source, S), (shift, C))[array_index]
        wide, deep = (OV + 1, HALO) if array_index == 0 else (OV, HALO - 1)
        from_rows, to_rows = rows_of(dy, deep)
        from_layers, to_layers = layers_of(dx, wide)
        return pltpu.make_async_remote_copy(
            src_ref=array.at[from_layers, from_rows],
            dst_ref=buf.at[to_layers, to_rows],
            send_sem=init_send.at[array_index, k],
            recv_sem=init_recv.at[array_index, k],
            device_id=device(dx, dy), device_id_type=MESH)

    even = lax.rem(b, 2) == 0
    odd = lax.rem(b, 2) == 1

    def all_initial(dirs, field_margin, start_it, send_wait=False):
        for array_index in range(3):
            for k in dirs:
                dx, dy = DIRECTIONS[k]
                if array_index == 0 and dx != 0 and not field_margin:
                    continue
                copy = initial(array_index, k)
                if start_it:
                    when_to(dy, copy.start)
                elif send_wait:
                    when_to(dy, copy.wait_send)
                else:
                    when_from(dy, copy.wait_recv)

    side_dirs, cross_dirs = (0, 1), (2, 4, 5, 3, 6, 7)
    side_cross = (cross_dirs[:3], cross_dirs[3:])

    lane = lax.broadcasted_iota(jnp.int32, (8, nz), 1)
    first_lane, last_lane = lane == 0, lane == nz - 1
    row = lax.broadcasted_iota(jnp.int32, (8, nz), 0)

    def weight(top):
        place = w * ny - HALO + top + row
        inside = jnp.logical_and(place >= 0, place < bands * ny)
        return jnp.where(inside, jnp.float32(1.0 / 56.0), jnp.float32(0.0))

    def filter_rows(ref, x, top):
        mid = ref[x, pl.ds(top, 8)]
        return (ref[x, pl.ds(top - 1, 8)] + ref[x, pl.ds(top + 1, 8)]) + (mid + mid)

    def stencil(ref, first, last, tops, emit):
        carry = []
        for top in tops:
            below, here = filter_rows(ref, first - 1, top), filter_rows(ref, first, top)
            carry += [below + here, here]

        def layer(x, carry):
            carry = list(carry)
            for t, top in enumerate(tops):
                pair, here = carry[2 * t], carry[2 * t + 1]
                above = filter_rows(ref, x + 1, top)
                next_pair = here + above
                both = pair + next_pair
                left = jnp.where(first_lane, 0.0, pltpu.roll(both, 1, 1))
                right = jnp.where(last_lane, 0.0, pltpu.roll(both, nz - 1, 1))
                emit(x, top, t, (both + both) + (left + right))
                carry[2 * t], carry[2 * t + 1] = next_pair, above
            return tuple(carry)

        whole = (last - first) // UNROLL

        def body(i, carry):
            for u in range(UNROLL):
                carry = layer(first + i * UNROLL + u, carry)
            return carry

        carry = lax.fori_loop(0, whole, body, tuple(carry))
        for x in range(first + whole * UNROLL, last):
            carry = layer(x, carry)

    wide_tops, own_tops = (1, 2 * HALO + ny - 9), (HALO,)
    wide_weights, own_weights = [weight(t) for t in wide_tops], [weight(t) for t in own_tops]

    def residual(first, last):
        def emit(x, top, t, filtered):
            here = pl.ds(top, 8)
            R0[x, here] = (S[x, here] - (centre_weight + C[x, here]) * F[x, here]) + wide_weights[t] * filtered
        stencil(F, first, last, wide_tops, emit)

    def pass_one(first, last):
        p, q = terms[0]
        def emit(x, top, t, filtered):
            here = pl.ds(top, 8)
            r = R0[x, here]
            image = (centre_weight + C[x, here]) * r - wide_weights[t] * filtered
            r1 = r - inv_c * image
            R1[x, here] = r1
            D1[x, here] = (p * inv_c) * r + q * r1
        stencil(R0, first, last, wide_tops, emit)

    def pass_two(first, last):
        p, q = terms[1]
        def emit(x, top, t, filtered):
            here = pl.ds(top, 8)
            d = D1[x, here]
            r2 = R1[x, here] - ((centre_weight + C[x, here]) * d - wide_weights[t] * filtered)
            R2[x, here] = r2
            D2[x, here] = p * d + q * r2
        stencil(D1, first, last, wide_tops, emit)

    def pass_three(first, last):
        p, q = terms[2]
        def emit(x, top, t, filtered):
            here = pl.ds(top, 8)
            d = D2[x, here]
            r3 = R2[x, here] - ((centre_weight + C[x, here]) * d - own_weights[t] * filtered)
            update = (inv_c * R0[x, here] + D1[x, here]) + (d + (p * d + q * r3))
            F[x, here] = F[x, here] + update
        stencil(D2, first, last, own_tops, emit)

    end = n + 2 * base - 1
    inner = 2 * OV + 2
    outer = end + 1 - inner

    def solve_inside():
        residual(inner, outer)
        pass_one(inner + 1, outer - 1)
        pass_two(inner + 2, outer - 2)
        pass_three(inner + 3, outer - 3)

    def solve_edge(side):
        for k, run in enumerate((residual, pass_one, pass_two, pass_three)):
            if side == 0:
                run(1, inner + k)
            else:
                run(outer - k, end)

    def across(e, side):
        dx = 1 if side == 0 else -1
        begin = base + n - OV - 1 if dx > 0 else 1
        return pltpu.make_async_remote_copy(
            src_ref=F.at[pl.ds(begin, edge), pl.ds(HALO, ny)],
            dst_ref=X.at[2 * e + side, :, pl.ds(HALO, ny)],
            send_sem=x_send.at[e, side], recv_sem=x_recv.at[e, side],
            device_id=device(dx, 0), device_id_type=MESH)

    def forward(e, side, dy):
        from_row = HALO + ny - HALO if dy > 0 else HALO
        to_row = 0 if dy > 0 else HALO + ny
        k = 2 * side + (0 if dy > 0 else 1)
        return pltpu.make_async_remote_copy(
            src_ref=X.at[2 * e + side, :, pl.ds(from_row, HALO)],
            dst_ref=X.at[2 * e + side, :, pl.ds(to_row, HALO)],
            send_sem=f_send.at[e, k], recv_sem=f_recv.at[e, k],
            device_id=device(0, dy), device_id_type=MESH)

    keep = n - 2 * OV

    def along(e, dy):
        from_row = HALO + ny - HALO if dy > 0 else HALO
        to_row = 0 if dy > 0 else HALO
        k = 0 if dy > 0 else 1
        return pltpu.make_async_remote_copy(
            src_ref=F.at[pl.ds(base + OV, keep), pl.ds(from_row, HALO)],
            dst_ref=Y.at[e, :, pl.ds(to_row, HALO)],
            send_sem=y_send.at[e, k], recv_sem=y_recv.at[e, k],
            device_id=device(0, dy), device_id_type=MESH)

    def last_copy(side):
        dx = 1 if side == 0 else -1
        begin = base + n if dx > 0 else base - OV
        return pltpu.make_async_remote_copy(
            src_ref=F.at[pl.ds(begin, OV), pl.ds(HALO, ny)],
            dst_ref=X.at[side + 2 * (2 * SWEEPS - 1), pl.ds(0, OV), pl.ds(HALO, ny)],
            send_sem=last_send.at[side], recv_sem=last_recv.at[side],
            device_id=device(dx, 0), device_id_type=MESH)

    def send_halo(e):
        if e < 2 * SWEEPS - 2:
            for dy in (1, -1):
                when_to(dy, along(e, dy).start)

    def finish_sends(e):
        for side in (0, 1):
            across(e, side).wait_send()
        if e < 2 * SWEEPS - 2:
            for dy in (1, -1):
                when_to(dy, along(e, dy).wait_send)

    def take_halo(e):
        for dy in (1, -1):
            when_from(dy, along(e, dy).wait_recv)

        def body(i, carry):
            F[base + OV + i, pl.ds(0, HALO)] = Y[e, i, pl.ds(0, HALO)]
            F[base + OV + i, pl.ds(HALO + ny, HALO)] = Y[e, i, pl.ds(HALO, HALO)]
            return carry
        lax.fori_loop(0, keep, body, 0)

    def send_side(e, side):
        across(e, 1 - side).start()

    def pass_margin_on(e, side):
        across(e, side).wait_recv()
        for dy in (1, -1):
            when_to(dy, forward(e, side, dy).start)

    def take_margin(e, side):
        for dy in (1, -1):
            when_from(dy, forward(e, side, dy).wait_recv)
        begin = 0 if side == 0 else base + n - OV
        for i in range(edge):
            F[begin + i] = X[2 * e + side, i]

    def margins_done(e):
        for side in (0, 1):
            for dy in (1, -1):
                when_to(dy, forward(e, side, dy).wait_send)

    def step(e, order, send):
        for side in order:
            pass_margin_on(e - 1, side)
        for side in order:
            take_margin(e - 1, side)
            solve_edge(side)
            send(side)

    def write_out(first, count, k):
        return pltpu.make_async_copy(
            F.at[pl.ds(base + first, count), pl.ds(HALO, ny)],
            out.at[pl.ds(first, count)], out_sem.at[k])

    all_initial(side_dirs, True, True)

    @pl.when(even)
    def _():
        all_initial(cross_dirs, False, True)
        for copy in own:
            copy.wait()
        all_initial(side_dirs, True, False)
        solve_inside()
        for side in (0, 1):
            all_initial(side_cross[side], True, False)
            solve_edge(side)
            send_side(0, side)
        send_halo(0)
        all_initial(side_dirs, True, False, True)
        all_initial(cross_dirs, False, False, True)
        for sweep in range(1, SWEEPS):
            e = 2 * sweep
            finish_sends(e - 2)
            take_halo(e - 2)
            solve_inside()
            step(e, (0, 1), lambda side: send_side(e, side))
            send_halo(e)
            margins_done(e - 1)
        finish_sends(2 * SWEEPS - 2)
        middle = write_out(OV, n - 2 * OV, 0)
        middle.start()
        for side in (0, 1):
            last_copy(side).wait_recv()

        def body(i, carry):
            here = pl.ds(HALO, ny)
            F[base + i, here] = X[2 * (2 * SWEEPS - 1), i, here]
            F[base + n - OV + i, here] = X[2 * (2 * SWEEPS - 1) + 1, i, here]
            return carry
        lax.fori_loop(0, OV, body, 0)
        low, high = write_out(0, OV, 1), write_out(n - OV, OV, 2)
        low.start()
        high.start()
        middle.wait()
        low.wait()
        high.wait()

    @pl.when(odd)
    def _():
        for side in (0, 1):
            all_initial(side_cross[side], True, True)
        for copy in own:
            copy.wait()
        all_initial(side_dirs, True, False)
        solve_inside()
        all_initial(cross_dirs, False, False)
        all_initial(side_dirs, True, False, True)
        all_initial(cross_dirs, True, False, True)
        for sweep in range(SWEEPS):
            e = 2 * sweep + 1
            if sweep > 0:
                finish_sends(e - 2)
                take_halo(e - 2)
                solve_inside()
            if sweep < SWEEPS - 1:
                step(e, (1, 0), lambda side: send_side(e, side))
                send_halo(e)
            else:
                step(e, (1, 0), lambda side: last_copy(1 - side).start())
            margins_done(e - 1)
        whole = write_out(0, n, 0)
        whole.start()
        for side in (0, 1):
            last_copy(side).wait_send()
        whole.wait()


def per_device(source, shift, start_field):
    n, ny, nz = source.shape
    layers, rows = n + 2 * OV + 2, ny + 2 * HALO
    work = pltpu.VMEM((layers, rows, nz), jnp.float32)
    dma = pltpu.SemaphoreType.DMA
    phases = 2 * SWEEPS
    return pl.pallas_call(
        kernel,
        out_shape=jax.ShapeDtypeStruct(source.shape, source.dtype),
        in_specs=[pl.BlockSpec(memory_space=pl.ANY)] * 3,
        out_specs=pl.BlockSpec(memory_space=pl.ANY),
        scratch_shapes=[work] * 8 + [
            pltpu.VMEM((2 * phases, 2 * OV + 1, rows, nz), jnp.float32),
            pltpu.VMEM((phases - 2, n - 2 * OV, 2 * HALO, nz), jnp.float32),
            dma((3,)), dma((3,)),
            dma((3, 8)), dma((3, 8)),
            dma((phases - 1, 2)), dma((phases - 1, 2)),
            dma((phases - 1, 4)), dma((phases - 1, 4)),
            dma((phases - 2, 2)), dma((phases - 2, 2)),
            dma((2,)), dma((2,)),
        ],
        compiler_params=pltpu.CompilerParams(
            collective_id=0, has_side_effects=True, vmem_limit_bytes=58 * 2**20),
    )(source, shift, start_field)


def solution(mesh):
    placed = P("blk", "narrow", None)
    return jax.shard_map(
        per_device, mesh=mesh, in_specs=(placed,) * 3, out_specs=placed, check_vma=False
    )
```
